128 devices in a mesh: row: 4 (over x_lo, core), col: 32 (over y, z, x_hi).
Axes of the slice: x: 4 (x_hi: 2, x_lo: 2; x = x_hi * 2 + x_lo), y: 4, z: 4, core: 2. Of those that a mesh axis runs over, the one named last changes fastest.
Arguments:
- x2_rows: bfloat16 [8192, 2048], P(('row', 'col')), may hold values from -0.21875 to 0.21875
- x_panels: bfloat16 [4, 512, 45056], P('row', None, 'col'), may hold values from -6 to 6
- panel_mask: int32 [4, 4, 352], P('row', None, 'col'), may hold values 0 or 1
- owners: int32 [4], replicated, may hold values from 0 to 3, each once
- x2_tile: bfloat16 [8192, 45056], P('row', 'col'), may hold values from -3 to 3
- block_ids: int32 [6144], P(('row', 'col')), may hold values from 0 to 175, as said below
- dest: int32 [6144, 1], P(('row', 'col')), may hold values from 0 to 31; in each aligned block of 48 rows (0 to 47, 48 to 95, ...) at most 2 rows name the same one
- counts: int32 [128], P(('row', 'col')), may hold values from 24 to 48
Outputs:
- purified: bfloat16 [8192, 128, 128], P(('row', 'col'))
The draws below stay inside these ranges and needn't reach their ends.
Inputs may be any that keep to these rules, and one draw needn't show every extreme that they name: `block_ids`: no two of one device's 48 entries are equal. `dest`: among one device's 48 entries no owner is named more than 2 times. `owners`: each slot is named once.
All inputs are finite; a program needn't handle non-finite values. No bound on the sum of `panel_mask` on one device may be relied on, other than what follows from the above.
Results may differ from the reference program's by a relative error of at most 0.001.
Values may be sent and summed in bfloat16 or wider, within the bound.
A program may use at most 128 MiB of HBM per device.

```python
import math
import jax
import jax.numpy as jnp
import numpy as np
from jax import lax

BS = 128
CB_DEV = 11
RB_DEV = 16
PB = 4
BLK_DEV = 48
CAP = 2
NR = 64
NC = 352
DEPTH = 16
N_ROW = 4
N_COL = 32


def draw_block_ids(key, part):
    key = jax.random.fold_in(key, 11)
    total = RB_DEV * CB_DEV
    devices = N_ROW * N_COL
    keys = jax.random.split(key, devices)
    perms = jax.vmap(lambda single: jax.random.permutation(single, total))(keys)
    listed = perms[:, :BLK_DEV].astype(jnp.int32)
    first_row = listed[0]
    holds_top = jnp.any(first_row == total - 1)
    first_row = jnp.where(holds_top, first_row, first_row.at[0].set(total - 1))
    listed = listed.at[0].set(first_row)
    return listed.reshape(-1).astype(jnp.int32)


def draw_counts(key, part):
    key = jax.random.fold_in(key, 23)
    devices = N_ROW * N_COL
    key_a, key_b, key_c = jax.random.split(key, 3)
    values = jax.random.randint(key_a, (devices,), BLK_DEV // 2, BLK_DEV + 1)
    top_index = jax.random.randint(key_b, (), 0, devices)
    low_index = (top_index + 1 + jax.random.randint(key_c, (), 0, devices - 1)) % devices
    values = values.at[top_index].set(BLK_DEV).at[low_index].set(BLK_DEV // 2)
    return values.astype(jnp.int32)


def with_ends(values, stream_key, smallest, largest):
    longest = values.shape.index(max(values.shape))
    spots = []
    for shift in (0, 1):
        where = [jax.random.randint(jax.random.fold_in(stream_key, axis), (), 0, length) for axis, length in enumerate(values.shape)]
        where[longest] = (where[longest] + shift) % values.shape[longest]
        spots.append(tuple(where))
    return values.at[spots[0]].set(smallest).at[spots[1]].set(largest)


def steps_of(key, extent, cuts, low, largest):
    def one(dim, blocks):
        draws = jax.random.uniform(jax.random.fold_in(jax.random.fold_in(key, 6), dim), (blocks,), jnp.float32, low / len(cuts), largest / len(cuts))
        return jnp.repeat(jnp.exp(draws), extent[dim] // blocks).reshape((-1,) + (1,) * (len(extent) - dim - 1))

    factor_of = one(*cuts[0])
    for cut in cuts[1:]:
        factor_of = factor_of * one(*cut)
    return factor_of


def assign_block(key, own, number, rows, amount, top, bound, lean):
    order = jax.random.permutation(key, amount)
    heavy_load, usual = shares(amount, rows * top, bound, lean, True), shares(amount, rows * top, bound, lean, False)
    places = jnp.arange(amount)

    def named(sizes, turn):
        used = int((sizes > 0).sum())
        fixed = max(1, used // 4)
        shifted = fixed + (places - fixed + turn * (used - fixed)) % max(1, amount - fixed)
        return jnp.zeros((amount,), jnp.int32).at[order[jnp.where(places < fixed, places, shifted)]].set(jnp.asarray(sizes, jnp.int32))

    sizes = jnp.where(number % 4 == 0, named(heavy_load, number // 4), named(usual, number - number // 4 - 1))
    mixed = jax.random.permutation(jax.random.fold_in(own, 3), amount)
    giver, taker = mixed[0:amount // 2 * 2:2], mixed[1:amount // 2 * 2:2]
    room = jnp.minimum(sizes[giver] - 1, bound - sizes[taker]) // 2
    room = jnp.where((giver == order[0]) | (taker == order[0]) | (sizes[taker] == 0), 0, jnp.maximum(room, 0))
    shifted = jax.random.randint(jax.random.fold_in(own, 4), (amount // 2,), 0, 1 << 20) % (room + 1)
    sizes = sizes.at[giver].add(-shifted).at[taker].add(shifted)
    labels = jnp.searchsorted(jnp.cumsum(sizes), jnp.arange(rows * top), side="right").astype(jnp.int32)
    table = labels.reshape(top, rows).T
    table = table[jax.random.permutation(jax.random.fold_in(own, 1), rows)]
    turn = jax.random.randint(jax.random.fold_in(own, 2), (rows, 1), 0, top)
    return jnp.take_along_axis(table, (jnp.arange(top)[None, :] + turn) % top, axis=1)


def shares(count, total, most, slope, full):
    portions = [(1 << 20) // math.isqrt(standing ** slope) + 1 for standing in range(1, count + 1)]
    largest = most if full else min(most, max(-(-total // count), total * portions[0] // sum(portions)))
    least = 1 if total - largest >= count - 1 else 0
    given, surplus = [largest] + [least] * (count - 1), total - largest - least * (count - 1)
    while surplus > 0:
        free = [i for i in range(1, count) if given[i] < largest] or [i for i in range(1, count) if given[i] < most]
        mass, remaining = sum([portions[i] for i in free]), surplus
        for i in free:
            extra = min(most - given[i], max(1, remaining * portions[i] // mass), surplus)
            given[i] = given[i] + extra
            surplus = surplus - extra
    return np.array(given)


def gaussian(stream_key, dims, spread, reach, shards=(), kind=jnp.bfloat16):
    values = jax.random.normal(stream_key, dims, jnp.float32) * spread
    if len(shards) > 0:
        values = steps_of(stream_key, dims, shards, -0.22, 0.18) * values
    return jnp.clip(values, min=-reach, max=reach).astype(kind)


def setup_inputs(seed: int = 0) -> dict:
    streams_of = jax.random.split(jax.random.key(seed), 9)
    x2_rows = gaussian(streams_of[0], (NR * BS, DEPTH * BS), (DEPTH * BS * 3 // 8) ** -0.5, 0.21875, ((0, 128),))
    x_panels = gaussian(streams_of[1], (N_ROW, PB * BS, NC * BS), 1.0, 6.0, ((0, 4), (2, 32)))
    panel_mask = with_ends((jax.random.randint(streams_of[2], (N_ROW, PB, NC), 0, 8) < 3).astype(jnp.int32), jax.random.fold_in(streams_of[2], 1), 0, 1)
    owners = jax.random.permutation(streams_of[3], N_ROW).astype(jnp.int32)
    x2_tile = gaussian(streams_of[4], (NR * BS, NC * BS), 0.5, 3.0, ((0, 4), (1, 32)))
    block_ids = draw_block_ids(jax.random.fold_in(streams_of[8], 71), 0)
    dest_keys = jax.random.split(jax.random.fold_in(streams_of[6], 1), (N_ROW * N_COL * BLK_DEV) // BLK_DEV)
    dest_turns = jax.random.permutation(jax.random.fold_in(streams_of[6], 3), (N_ROW * N_COL * BLK_DEV) // BLK_DEV)
    dest = jax.vmap(lambda own, number: assign_block(jax.random.fold_in(streams_of[6], 2), own, number, BLK_DEV, N_COL, 1, CAP, 2))(dest_keys, dest_turns).reshape((N_ROW * N_COL * BLK_DEV, 1))
    counts = draw_counts(jax.random.fold_in(streams_of[8], 71), 0)
    return dict(x2_rows=x2_rows, x_panels=x_panels, panel_mask=panel_mask, owners=owners, x2_tile=x2_tile, block_ids=block_ids, dest=dest, counts=counts)


def tile_blocks(square_tile):
    shaped = square_tile.reshape(RB_DEV, BS, CB_DEV, BS).transpose(0, 2, 1, 3)
    return shaped.reshape(RB_DEV * CB_DEV, BS, BS)


def reference(x2_rows, x_panels, panel_mask, owners, x2_tile, block_ids, dest, counts):
    devices = N_ROW * N_COL
    depth = DEPTH * BS
    cell_mask = jnp.broadcast_to(panel_mask[:, :, None, :, None], (N_ROW, PB, BS, NC, BS))
    cell_mask = cell_mask.reshape(N_ROW, PB * BS, NC * BS).astype(jnp.bfloat16)
    masked = x_panels * cell_mask
    ordered = jnp.take(masked, owners, axis=0).reshape(depth, NC * BS)
    entry_ids = block_ids.reshape(devices, BLK_DEV)

    def one_device(device):
        row_group = device // N_COL
        col_group = device % N_COL
        row_slab = lax.dynamic_slice_in_dim(x2_rows, row_group * (RB_DEV * BS), RB_DEV * BS, 0)
        col_slab = lax.dynamic_slice_in_dim(ordered, col_group * (CB_DEV * BS), CB_DEV * BS, 1)
        square_tile = lax.dynamic_slice(x2_tile, (row_group * (RB_DEV * BS), col_group * (CB_DEV * BS)), (RB_DEV * BS, CB_DEV * BS))
        listed = lax.dynamic_index_in_dim(entry_ids, device, 0, keepdims=False)
        left_rows = jnp.take(row_slab.reshape(RB_DEV, BS, depth), listed // CB_DEV, axis=0).astype(jnp.float32)
        right_cols = jnp.take(col_slab.reshape(depth, CB_DEV, BS).transpose(1, 0, 2), listed % CB_DEV, axis=0).astype(jnp.float32)
        cube_term = jnp.einsum("eik,ekj->eij", left_rows, right_cols)
        square_term = jnp.take(tile_blocks(square_tile), listed, axis=0).astype(jnp.float32)
        alive_mask = jnp.arange(BLK_DEV, dtype=jnp.int32) < lax.dynamic_index_in_dim(counts, device, 0, keepdims=False)
        result = jnp.where(alive_mask[:, None, None], 3.0 * square_term - 2.0 * cube_term, jnp.zeros_like(cube_term))
        return result.astype(jnp.bfloat16)

    blocks = lax.map(one_device, jnp.arange(devices, dtype=jnp.int32))
    owner_cols = dest.reshape(devices, BLK_DEV)
    one_hot = (owner_cols[:, :, None] == jnp.arange(N_COL, dtype=jnp.int32)[None, None, :]).astype(jnp.int32)
    slot_rank = jnp.sum((jnp.cumsum(one_hot, axis=1) - one_hot) * one_hot, axis=2)
    sender = jnp.arange(devices, dtype=jnp.int32)[:, None]
    row_group = sender // N_COL
    col_group = sender % N_COL
    position = ((row_group * N_COL + owner_cols) * N_COL + col_group) * CAP + slot_rank
    purified = jnp.zeros((devices * N_COL * CAP, BS, BS), jnp.bfloat16)
    purified = purified.at[position.reshape(-1)].set(blocks.reshape(devices * BLK_DEV, BS, BS))
    return purified
```

```python
import functools

import jax
import jax.numpy as jnp
from jax import lax
from jax.experimental import pallas as pl
from jax.experimental.pallas import tpu as pltpu
from jax.sharding import PartitionSpec as P

MESH = pl.DeviceIdType.MESH
BS = 128
CB = 11
RB = 16
PB = 4
DEPTH = 2048
HALF = DEPTH // 2
NCOL = 32
SHARD = 64
PARTS = 4
UNIT = SHARD // PARTS
SLOTS = 2
PANEL_CUTS = (0, 3, 6, 9, 11)
PANEL_PARTS = len(PANEL_CUTS) - 1


def kernel(
    table_ref, owners_ref, mask_ref, rows_hbm, panel_hbm, tile_hbm, out_ref,
    rows, panels, panel_in, tile, staged,
    load_sem, unit_send, unit_recv, panel_send, panel_recv, out_send, out_recv, self_sem,
):
    row = lax.axis_index("row")
    col = lax.axis_index("col")
    y, z, h = col // 8, (col // 2) % 4, col % 2
    x_lo, core = row // 2, row % 2

    def peer(dy, dz, dh):
        return ((y + dy + 4) % 4) * 8 + ((z + dz + 4) % 4) * 2 + (h + dh) % 2

    beside = (1 - x_lo) * 2 + core
    other_core = x_lo * 2 + 1 - core

    own = rows.at[col // 2, pl.ds(pl.multiple_of(h * SHARD, SHARD), SHARD)]
    loads = [
        pltpu.make_async_copy(rows_hbm, own, load_sem.at[0]),
        pltpu.make_async_copy(panel_hbm.at[0], panel_in, load_sem.at[1]),
    ]
    for c in range(CB):
        loads.append(
            pltpu.make_async_copy(
                tile_hbm.at[:, :, pl.ds(c * BS, BS)], tile.at[c], load_sem.at[2 + c]
            )
        )
    for load in loads:
        load.start()

    barrier = pltpu.get_barrier_semaphore()

    def greet(n, carry):
        pl.semaphore_signal(
            barrier, inc=1, device_id=(row, (col + n) % NCOL), device_id_type=MESH
        )
        return carry

    lax.fori_loop(1, NCOL, greet, 0)
    pl.semaphore_signal(barrier, inc=1, device_id=(beside, col), device_id_type=MESH)
    pl.semaphore_signal(barrier, inc=1, device_id=(other_core, col), device_id_type=MESH)
    pl.semaphore_wait(barrier, NCOL + 1)

    sends = []

    def unit_view(q, source, half):
        lines = pl.ds(pl.multiple_of(source % 2 * SHARD + q * UNIT, UNIT), UNIT)
        if half is None:
            return rows.at[source // 2, lines]
        return rows.at[source // 2, lines, pl.ds(half * HALF, HALF)]

    def send(q, unit, to, half=None):
        source = peer(*unit)
        view = unit_view(q, source, half)
        copy = pltpu.make_async_remote_copy(
            src_ref=view,
            dst_ref=view,
            send_sem=unit_send.at[len(sends)],
            recv_sem=unit_recv.at[q, source, half or 0],
            device_id=(row, peer(*to)),
            device_id_type=MESH,
        )
        copy.start()
        sends.append(copy)

    def arrived(q, unit, half=None):
        source = peer(*unit)
        view = unit_view(q, source, half)
        pltpu.make_async_remote_copy(
            src_ref=view,
            dst_ref=view,
            send_sem=unit_send.at[0],
            recv_sem=unit_recv.at[q, source, half or 0],
            device_id=(row, col),
            device_id_type=MESH,
        ).wait_recv()

    def along(axis, step):
        return (step, 0, 0) if axis == 0 else (0, step, 0)

    def unit_at(fast, first, second):
        return (first, second, 0) if fast == 0 else (second, first, 1)

    def both_ways(q, fast, unit, axis, half=None):
        send(q, unit, along(axis, 1), half)
        send(q, unit, along(axis, -1), half)

    def stage0(q):
        send(q, (0, 0, 0), (0, 0, 1))
        both_ways(q, 0, (0, 0, 0), 0)
        both_ways(q, 0, (0, 0, 0), 1)

    def forward(q, unit, axis, came):
        send(q, unit, along(axis, -came), 0 if came < 0 else 1)

    def stage1(q):
        arrived(q, (0, 0, 1))
        both_ways(q, 1, (0, 0, 1), 1)
        both_ways(q, 1, (0, 0, 1), 0)
        for came in (-1, 1):
            unit = unit_at(0, came, 0)
            arrived(q, unit)
            forward(q, unit, 0, came)
            both_ways(q, 0, unit, 1)

    def stage2(q):
        for came in (-1, 1):
            unit = unit_at(0, 0, came)
            arrived(q, unit)
            forward(q, unit, 1, came)
        for came in (-1, 1):
            unit = unit_at(1, came, 0)
            arrived(q, unit)
            forward(q, unit, 1, came)
            both_ways(q, 1, unit, 0)
        for came in (-1, 1):
            unit = unit_at(1, 0, came)
            arrived(q, unit)
            forward(q, unit, 0, came)

    def stage3(q):
        for fast in (0, 1):
            for half in (0, 1):
                unit = unit_at(fast, 2, 0)
                arrived(q, unit, half)
                both_ways(q, fast, unit, 1 - fast, half)
        for fast in (0, 1):
            for first in (-1, 1):
                for came in (-1, 1):
                    unit = unit_at(fast, first, came)
                    arrived(q, unit)
                    forward(q, unit, 1 - fast, came)

    def stage4(q):
        for fast in (0, 1):
            for came in (-1, 1):
                unit = unit_at(fast, 2, came)
                for half in (0, 1):
                    arrived(q, unit, half)
                forward(q, unit, 1 - fast, came)

    def stage5(q):
        for fast in (0, 1):
            for first in (0, -1, 1, 2):
                for half in (0, 1):
                    arrived(q, unit_at(fast, first, 2), half)

    panel_sends = []

    def panel_copy(part, slot, kind, to):
        first, last = PANEL_CUTS[part], PANEL_CUTS[part + 1]
        view = panels.at[slot, pl.ds(first, last - first)]
        return pltpu.make_async_remote_copy(
            src_ref=view,
            dst_ref=view,
            send_sem=panel_send.at[kind, part],
            recv_sem=panel_recv.at[kind, part],
            device_id=(to, col),
            device_id_type=MESH,
        )

    def start_panels():
        for part in range(PANEL_PARTS):
            copy = panel_copy(part, row, 0, beside)
            copy.start()
            panel_sends.append(copy)
        for part in range(PANEL_PARTS):
            copy = panel_copy(part, row, 1, other_core)
            copy.start()
            panel_sends.append(copy)

    def pass_panel(part):
        panel_copy(part, beside, 0, beside).wait_recv()
        copy = panel_copy(part, beside, 2, other_core)
        copy.start()
        panel_sends.append(copy)

    stages = [stage0, stage1, stage2, stage3, stage4, stage5]

    loads[0].wait()
    stage0(0)

    loads[1].wait()
    for p in range(PB):
        for c in range(CB):
            factor = mask_ref[0, p, c].astype(jnp.float32)
            block = panel_in[p * BS : (p + 1) * BS, c * BS : (c + 1) * BS]
            panels[row, c, p * BS : (p + 1) * BS] = (
                block.astype(jnp.float32) * factor
            ).astype(jnp.bfloat16)
    start_panels()

    for step in range(1, PARTS + len(stages) - 1):
        for q in range(PARTS):
            if 0 <= step - q < len(stages):
                stages[step - q](q)
        if step >= 4 and step - 4 < PANEL_PARTS:
            pass_panel(step - 4)
    for part in range(PANEL_PARTS):
        panel_copy(part, other_core, 1, other_core).wait_recv()
    for part in range(PANEL_PARTS):
        panel_copy(part, (1 - x_lo) * 2 + 1 - core, 2, other_core).wait_recv()
    for load in loads[2:]:
        load.wait()

    def product(slot):
        i = table_ref[0, slot]
        j = table_ref[1, slot]
        live = table_ref[2, slot].astype(jnp.float32)
        cube = jnp.zeros((BS, BS), jnp.float32)
        for k in range(4):
            cube = cube + jnp.dot(
                rows[i, :, k * PB * BS : (k + 1) * PB * BS],
                panels[owners_ref[k], j],
                preferred_element_type=jnp.float32,
            )
        square = tile[j, i].astype(jnp.float32)
        return ((3.0 * square - 2.0 * cube) * live).astype(jnp.bfloat16)

    def owner_of(n):
        return peer(n // 8, (n // 2) % 4, n % 2)

    def source_of(n):
        return peer(4 - n // 8, 4 - (n // 2) % 4, n % 2)

    def make(n):
        owner = owner_of(n)
        for s in range(SLOTS):
            staged[n, s] = product(owner * SLOTS + s)
        return owner

    def out_copy(n, owner, at):
        return pltpu.make_async_remote_copy(
            src_ref=staged.at[n],
            dst_ref=out_ref.at[pl.ds(at * SLOTS, SLOTS)],
            send_sem=out_send.at[n],
            recv_sem=out_recv.at[n],
            device_id=(row, owner),
            device_id_type=MESH,
        )

    def exchange(n, carry):
        owner = make(n)
        out_copy(n, owner, col).start()
        return carry

    lax.fori_loop(1, NCOL, exchange, 0)
    make(0)
    keep = pltpu.make_async_copy(
        staged.at[0], out_ref.at[pl.ds(col * SLOTS, SLOTS)], self_sem.at[0]
    )
    keep.start()

    for copy in sends:
        copy.wait_send()
    for copy in panel_sends:
        copy.wait_send()

    def finish(n, carry):
        out_copy(n, owner_of(n), col).wait_send()
        out_copy(n, owner_of(n), source_of(n)).wait_recv()
        return carry

    lax.fori_loop(1, NCOL, finish, 0)
    keep.wait()


def slot_table(block_ids, dest, counts):
    count = block_ids.shape[0]
    owner = dest[:, 0]
    entry = jnp.arange(count, dtype=jnp.int32)
    same = (owner[:, None] == owner[None, :]) & (entry[None, :] < entry[:, None])
    slot = owner * SLOTS + jnp.sum(same.astype(jnp.int32), axis=1)
    live = (entry < counts[0]).astype(jnp.int32)
    block_row = block_ids // CB
    values = jnp.stack([block_row, block_ids - block_row * CB, live])
    at = slot[None, :] == jnp.arange(NCOL * SLOTS, dtype=jnp.int32)[:, None]
    return jnp.sum(jnp.where(at[None], values[:, None, :], 0), axis=2)


def shards(x2_rows, x_panels, panel_mask, owners, x2_tile, block_ids, dest, counts):
    sem = pltpu.SemaphoreType.DMA
    return pl.pallas_call(
        kernel,
        out_shape=jax.ShapeDtypeStruct((NCOL * SLOTS, BS, BS), jnp.bfloat16),
        in_specs=[pl.BlockSpec(memory_space=pltpu.SMEM)] * 3
        + [pl.BlockSpec(memory_space=pl.ANY)] * 3,
        out_specs=pl.BlockSpec(memory_space=pl.ANY),
        scratch_shapes=[
            pltpu.VMEM((RB, BS, DEPTH), jnp.bfloat16),
            pltpu.VMEM((4, CB, PB * BS, BS), jnp.bfloat16),
            pltpu.VMEM((PB * BS, CB * BS), jnp.bfloat16),
            pltpu.VMEM((CB, RB, BS, BS), jnp.bfloat16),
            pltpu.VMEM((NCOL, SLOTS, BS, BS), jnp.bfloat16),
            sem((2 + CB,)),
            sem((PARTS * 56,)),
            sem((PARTS, NCOL, 2)),
            sem((3, PANEL_PARTS)),
            sem((3, PANEL_PARTS)),
            sem((NCOL,)),
            sem((NCOL,)),
            sem((1,)),
        ],
        compiler_params=pltpu.CompilerParams(
            collective_id=0, has_side_effects=True, vmem_limit_bytes=48 * 2**20
        ),
        cost_estimate=pl.CostEstimate(
            flops=4_300_000_000, bytes_accessed=12_000_000, transcendentals=0
        ),
    )(
        slot_table(block_ids, dest, counts),
        owners,
        panel_mask,
        x2_rows,
        x_panels,
        x2_tile.reshape(RB, BS, CB * BS),
    )


def solution(mesh):
    return jax.shard_map(
        shards,
        mesh=mesh,
        in_specs=(
            P(("row", "col"), None),
            P("row", None, "col"),
            P("row", None, "col"),
            P(),
            P("row", "col"),
            P(("row", "col")),
            P(("row", "col"), None),
            P(("row", "col")),
        ),
        out_specs=P(("row", "col"), None, None),
        check_vma=False,
    )
```

```python
import functools

import jax
import jax.numpy as jnp
from jax import lax
from jax.experimental import pallas as pl
from jax.experimental.pallas import tpu as pltpu
from jax.sharding import PartitionSpec as P

MESH = pl.DeviceIdType.MESH
BS = 128
CB = 11
RB = 16
PB = 4
DEPTH = 2048
HALF = DEPTH // 2
NCOL = 32
SHARD = 64
PARTS = 1
UNIT = SHARD // PARTS
SLOTS = 2
PANEL_CUTS = (0, 3, 6, 9, 11)
PANEL_PARTS = len(PANEL_CUTS) - 1


def kernel(
    ids_hbm, dest_hbm, counts_hbm, owners_hbm, mask_hbm, rows_hbm, panel_hbm, tile_hbm, out_ref,
    rows, panels, panel_in, tile, staged, ids, dest, table,
    counts_ref, owners_ref, mask_ref, table_ref,
    load_sem, ring_send, pair_send, pair_recv, unit_recv, panel_send, panel_recv, out_send, out_recv,
):
    row = lax.axis_index("row")
    col = lax.axis_index("col")
    y, z, h = col // 8, (col // 2) % 4, col % 2
    x_lo, core = row // 2, row % 2

    def peer(dy, dz, dh):
        return ((y + dy + 4) % 4) * 8 + ((z + dz + 4) % 4) * 2 + (h + dh) % 2

    beside = (1 - x_lo) * 2 + core
    other_core = x_lo * 2 + 1 - core

    own = rows.at[col // 2, pl.ds(pl.multiple_of(h * SHARD, SHARD), SHARD)]
    loads = [
        pltpu.make_async_copy(rows_hbm, own, load_sem.at[0]),
        pltpu.make_async_copy(panel_hbm.at[0], panel_in, load_sem.at[1]),
        pltpu.make_async_copy(mask_hbm, mask_ref, load_sem.at[2]),
        pltpu.make_async_copy(owners_hbm, owners_ref, load_sem.at[3]),
        pltpu.make_async_copy(counts_hbm, counts_ref, load_sem.at[4]),
        pltpu.make_async_copy(ids_hbm, ids, load_sem.at[5]),
        pltpu.make_async_copy(dest_hbm, dest, load_sem.at[6]),
    ]
    for c in range(CB):
        loads.append(
            pltpu.make_async_copy(
                tile_hbm.at[:, :, pl.ds(c * BS, BS)], tile.at[c], load_sem.at[7 + c]
            )
        )
    for load in loads:
        load.start()

    barrier = pltpu.get_barrier_semaphore()

    def greet(n, carry):
        pl.semaphore_signal(
            barrier, inc=1, device_id=(row, (col + n) % NCOL), device_id_type=MESH
        )
        return carry

    lax.fori_loop(1, NCOL, greet, 0)
    pl.semaphore_signal(barrier, inc=1, device_id=(beside, col), device_id_type=MESH)
    pl.semaphore_signal(barrier, inc=1, device_id=(other_core, col), device_id_type=MESH)
    pl.semaphore_wait(barrier, NCOL + 1)

    def fill_table():
        count = ids.shape[1]
        first = lax.broadcasted_iota(jnp.int32, (count, count), 0)
        second = lax.broadcasted_iota(jnp.int32, (count, count), 1)

        def upright(line):
            return jnp.sum(jnp.where(first == second, line, 0), axis=1, keepdims=True)

        owner, listed = upright(dest[...]), upright(ids[...])
        before = (owner == dest[...]) & (second < first)
        slot = owner * SLOTS + jnp.sum(before.astype(jnp.int32), axis=1, keepdims=True)
        hit = slot == lax.broadcasted_iota(jnp.int32, (count, table.shape[1]), 1)
        block_row = (listed * 745) >> 13
        entry = lax.broadcasted_iota(jnp.int32, (count, 1), 0)
        live = (entry < counts_ref[0]).astype(jnp.int32)
        table[...] = jnp.zeros_like(table)
        for n, column in enumerate((block_row, listed - block_row * CB, live)):
            table[n : n + 1] = jnp.sum(jnp.where(hit, column, 0), axis=0, keepdims=True)
        copy = pltpu.make_async_copy(table, table_ref, load_sem.at[0])
        copy.start()
        copy.wait()

    def place(unit):
        q, fast, first, second, dh = unit
        return peer(first, second, dh) if fast == 0 else peer(second, first, dh)

    def unit_view(unit, half):
        source = place(unit)
        width = HALF if half is None else HALF // 2
        start = unit[1] * HALF + (half or 0) * width
        lines = pl.ds(pl.multiple_of(source % 2 * SHARD + unit[0] * UNIT, UNIT), UNIT)
        return rows.at[source // 2, lines, pl.ds(start, width)]

    def unit_copy(unit, half, to):
        view = unit_view(unit, half)
        return pltpu.make_async_remote_copy(
            src_ref=view,
            dst_ref=view,
            send_sem=ring_send.at[0],
            recv_sem=unit_recv.at[unit[0], unit[1], place(unit), half or 0],
            device_id=(row, to),
            device_id_type=MESH,
        )

    def arrived(unit, half=None):
        unit_copy(unit, half, col).wait_recv()

    def along(axis, step):
        return peer(step, 0, 0) if axis == 0 else peer(0, step, 0)

    def both_ways(unit, axis, half=None):
        unit_copy(unit, half, along(axis, 1)).start()
        unit_copy(unit, half, along(axis, -1)).start()

    def forward(unit, axis, came):
        unit_copy(unit, 0 if came < 0 else 1, along(axis, -came)).start()

    def pair_copy(q, source):
        lines = pl.ds(pl.multiple_of(source % 2 * SHARD + q * UNIT, UNIT), UNIT)
        view = rows.at[source // 2, lines]
        return pltpu.make_async_remote_copy(
            src_ref=view,
            dst_ref=view,
            send_sem=pair_send.at[0],
            recv_sem=pair_recv.at[q],
            device_id=(row, peer(0, 0, 1)),
            device_id_type=MESH,
        )

    def stage0(q, dh):
        if dh:
            pair_copy(q, peer(0, 0, 1)).wait_recv()
        for fast in (0, 1):
            both_ways((q, fast, 0, 0, dh), fast)
        for fast in (0, 1):
            both_ways((q, fast, 0, 0, dh), 1 - fast)

    def stage1(q, dh):
        for came in (-1, 1):
            for fast in (0, 1):
                unit = (q, fast, came, 0, dh)
                arrived(unit)
                forward(unit, fast, came)
                both_ways(unit, 1 - fast)

    def stage2(q, dh):
        for came in (-1, 1):
            for fast in (0, 1):
                unit = (q, fast, 0, came, dh)
                arrived(unit)
                forward(unit, 1 - fast, came)
        for half in (0, 1):
            for fast in (0, 1):
                unit = (q, fast, 2, 0, dh)
                arrived(unit, half)
                both_ways(unit, 1 - fast, half)

    def stage3(q, dh):
        for first in (-1, 1):
            for came in (-1, 1):
                for fast in (0, 1):
                    unit = (q, fast, first, came, dh)
                    arrived(unit)
                    forward(unit, 1 - fast, came)

    def stage4(q, dh):
        for came in (-1, 1):
            for fast in (0, 1):
                unit = (q, fast, 2, came, dh)
                arrived(unit, 0)
                arrived(unit, 1)
                forward(unit, 1 - fast, came)

    def stage5(q, dh):
        for first in (0, -1, 1, 2):
            for fast in (0, 1):
                arrived((q, fast, first, 2, dh), 0)
                arrived((q, fast, first, 2, dh), 1)

    def panel_copy(part, slot, kind, to):
        first, last = PANEL_CUTS[part], PANEL_CUTS[part + 1]
        view = panels.at[slot, pl.ds(first, last - first)]
        return pltpu.make_async_remote_copy(
            src_ref=view,
            dst_ref=view,
            send_sem=panel_send.at[kind],
            recv_sem=panel_recv.at[kind, part],
            device_id=(to, col),
            device_id_type=MESH,
        )

    def start_panels():
        for part in range(PANEL_PARTS):
            panel_copy(part, row, 0, beside).start()

    def pass_panel(part):
        panel_copy(part, beside, 0, beside).wait_recv()
        panel_copy(part, beside, 2, other_core).start()

    loads[0].wait()
    for q in range(PARTS):
        pair_copy(q, col).start()
    for q in range(PARTS):
        stage0(q, 0)

    for load in loads[1:7]:
        load.wait()
    fill_table()
    for p in range(PB):
        for c in range(CB):
            factor = mask_ref[0, p, c].astype(jnp.float32)
            block = panel_in[p * BS : (p + 1) * BS, c * BS : (c + 1) * BS]
            panels[row, c, p * BS : (p + 1) * BS] = (
                block.astype(jnp.float32) * factor
            ).astype(jnp.bfloat16)
    for part in range(PANEL_PARTS):
        panel_copy(part, row, 1, other_core).start()
    for q in range(PARTS):
        stage0(q, 1)
    start_panels()
    for stage in (stage1, stage2, stage3, stage4):
        for dh in (0, 1):
            for q in range(PARTS):
                stage(q, dh)
    for part in range(PANEL_PARTS):
        pass_panel(part)
    for dh in (0, 1):
        for q in range(PARTS):
            stage5(q, dh)
    for part in range(PANEL_PARTS):
        panel_copy(part, other_core, 1, other_core).wait_recv()
    for part in range(PANEL_PARTS):
        panel_copy(part, (1 - x_lo) * 2 + 1 - core, 2, other_core).wait_recv()
    for load in loads[7:]:
        load.wait()

    def product(slot):
        i = table_ref[0, slot]
        j = table_ref[1, slot]
        live = table_ref[2, slot].astype(jnp.float32)
        cube = jnp.zeros((BS, BS), jnp.float32)
        for k in range(4):
            cube = cube + jnp.dot(
                rows[i, :, k * PB * BS : (k + 1) * PB * BS],
                panels[owners_ref[k], j],
                preferred_element_type=jnp.float32,
            )
        square = tile[j, i].astype(jnp.float32)
        return ((3.0 * square - 2.0 * cube) * live).astype(jnp.bfloat16)

    def owner_of(n):
        mixed = n * 11 % NCOL
        return peer(mixed // 8, mixed // 2 % 4, mixed % 2)

    def make(n):
        owner = owner_of(n)
        for s in range(SLOTS):
            staged[n, s] = product(owner * SLOTS + s)
        return owner

    mine = out_ref.at[pl.ds(col * SLOTS, SLOTS)]

    def give(n, owner):
        pltpu.make_async_remote_copy(
            src_ref=staged.at[n],
            dst_ref=mine,
            send_sem=out_send.at[0],
            recv_sem=out_recv.at[0],
            device_id=(row, owner),
            device_id_type=MESH,
        ).start()

    def exchange(pair, carry):
        n = 2 * pair + 1
        first, second = make(n), make(n + 1)
        give(n, first)
        give(n + 1, second)
        return carry

    lax.fori_loop(0, NCOL // 2 - 1, exchange, 0)
    last = make(NCOL - 1)
    make(0)
    give(NCOL - 1, last)
    keep = pltpu.make_async_copy(staged.at[0], mine, load_sem.at[1])
    keep.start()

    def await_bytes(ref, sem):
        pltpu.make_async_copy(ref, ref, sem).wait()

    await_bytes(rows.at[pl.ds(0, RB - 1)], ring_send.at[0])
    await_bytes(own, pair_send.at[0])
    for kind in range(3):
        await_bytes(panels.at[0], panel_send.at[kind])
    keep.wait()
    await_bytes(staged.at[pl.ds(1, NCOL - 1)], out_send.at[0])
    await_bytes(staged.at[pl.ds(1, NCOL - 1)], out_recv.at[0])


def shards(x2_rows, x_panels, panel_mask, owners, x2_tile, block_ids, dest, counts):
    sem = pltpu.SemaphoreType.DMA
    count = block_ids.shape[0]
    return pl.pallas_call(
        kernel,
        out_shape=jax.ShapeDtypeStruct((NCOL * SLOTS, BS, BS), jnp.bfloat16),
        in_specs=[pl.BlockSpec(memory_space=pltpu.HBM)] * 8,
        out_specs=pl.BlockSpec(memory_space=pl.ANY),
        scratch_shapes=[
            pltpu.VMEM((RB, BS, DEPTH), jnp.bfloat16),
            pltpu.VMEM((4, CB, PB * BS, BS), jnp.bfloat16),
            pltpu.VMEM((PB * BS, CB * BS), jnp.bfloat16),
            pltpu.VMEM((CB, RB, BS, BS), jnp.bfloat16),
            pltpu.VMEM((NCOL, SLOTS, BS, BS), jnp.bfloat16),
            pltpu.VMEM((1, count), jnp.int32),
            pltpu.VMEM((1, count), jnp.int32),
            pltpu.VMEM((8, BS), jnp.int32),
            pltpu.SMEM(counts.shape, jnp.int32),
            pltpu.SMEM(owners.shape, jnp.int32),
            pltpu.SMEM(panel_mask.shape, jnp.int32),
            pltpu.SMEM((8, BS), jnp.int32),
            sem((7 + CB,)),
            sem((1,)),
            sem((1,)),
            sem((PARTS,)),
            sem((PARTS, 2, NCOL, 2)),
            sem((3,)),
            sem((3, PANEL_PARTS)),
            sem((1,)),
            sem((1,)),
        ],
        compiler_params=pltpu.CompilerParams(
            collective_id=0, has_side_effects=True, vmem_limit_bytes=60 * 2**20
        ),
        cost_estimate=pl.CostEstimate(
            flops=4_300_000_000, bytes_accessed=12_000_000, transcendentals=0
        ),
    )(
        block_ids.reshape(1, count),
        dest.reshape(1, count),
        counts,
        owners,
        panel_mask,
        x2_rows,
        x_panels,
        x2_tile.reshape(RB, BS, CB * BS),
    )


def solution(mesh):
    return jax.shard_map(
        shards,
        mesh=mesh,
        in_specs=(
            P(("row", "col"), None),
            P("row", None, "col"),
            P("row", None, "col"),
            P(),
            P("row", "col"),
            P(("row", "col")),
            P(("row", "col"), None),
            P(("row", "col")),
        ),
        out_specs=P(("row", "col"), None, None),
        check_vma=False,
    )
```

```python
import functools

import jax
import jax.numpy as jnp
from jax import lax
from jax.experimental import pallas as pl
from jax.experimental.pallas import tpu as pltpu
from jax.sharding import PartitionSpec as P

MESH = pl.DeviceIdType.MESH
BS = 128
CB = 11
RB = 16
PB = 4
DEPTH = 2048
HALF = DEPTH // 2
NCOL = 32
SHARD = 64
PARTS = 1
UNIT = SHARD // PARTS
SLOTS = 2
PANEL_CUTS = (0, 3, 6, 9, 11)
PANEL_PARTS = len(PANEL_CUTS) - 1


def kernel(
    ids_hbm, dest_hbm, counts_hbm, owners_hbm, mask_hbm, rows_hbm, panel_hbm, tile_hbm, out_ref,
    rows, panels, panel_in, tile, staged, ids, dest, table,
    counts_ref, owners_ref, mask_ref, table_ref,
    load_sem, tile_sem, ring_send, pair_send, pair_recv, unit_recv, stay_recv, panel_send, panel_recv, out_send, out_recv,
):
    row = lax.axis_index("row")
    col = lax.axis_index("col")
    y, z, h = col // 8, (col // 2) % 4, col % 2
    x_lo, core = row // 2, row % 2

    def peer(dy, dz, dh):
        return ((y + dy + 4) % 4) * 8 + ((z + dz + 4) % 4) * 2 + (h + dh) % 2

    beside = (1 - x_lo) * 2 + core
    other_core = x_lo * 2 + 1 - core

    own = rows.at[col // 2, pl.ds(pl.multiple_of(h * SHARD, SHARD), SHARD)]
    load_rows = pltpu.make_async_copy(rows_hbm, own, load_sem.at[0])
    load_rows.start()

    barrier = pltpu.get_barrier_semaphore()

    def greet(n, carry):
        pl.semaphore_signal(
            barrier, inc=1, device_id=(row, (col + n) % NCOL), device_id_type=MESH
        )
        return carry

    lax.fori_loop(1, NCOL, greet, 0)
    pl.semaphore_signal(barrier, inc=1, device_id=(beside, col), device_id_type=MESH)
    pl.semaphore_signal(barrier, inc=1, device_id=(other_core, col), device_id_type=MESH)

    loads = [
        pltpu.make_async_copy(source, target, load_sem.at[n + 1])
        for n, (source, target) in enumerate(
            (
                (dest_hbm, dest),
                (ids_hbm, ids),
                (counts_hbm, counts_ref),
                (mask_hbm, mask_ref),
                (owners_hbm, owners_ref),
                (panel_hbm.at[0], panel_in),
            )
        )
    ]
    for load in loads:
        load.start()
    for c in range(CB):
        pltpu.make_async_copy(
            tile_hbm.at[:, :, pl.ds(c * BS, BS)], tile.at[c], tile_sem.at[0]
        ).start()
    pl.semaphore_wait(barrier, NCOL + 1)

    def await_bytes(ref, sem):
        pltpu.make_async_copy(ref, ref, sem).wait()

    def fill_table():
        count = ids.shape[1]
        first = lax.broadcasted_iota(jnp.int32, (count, count), 0)
        second = lax.broadcasted_iota(jnp.int32, (count, count), 1)

        def upright(line):
            return jnp.sum(jnp.where(first == second, line, 0), axis=1, keepdims=True)

        owner, listed = upright(dest[...]), upright(ids[...])
        before = (owner == dest[...]) & (second < first)
        slot = owner * SLOTS + jnp.sum(before.astype(jnp.int32), axis=1, keepdims=True)
        hit = slot == lax.broadcasted_iota(jnp.int32, (count, table.shape[1]), 1)
        block_row = (listed * 745) >> 13
        entry = lax.broadcasted_iota(jnp.int32, (count, 1), 0)
        live = (entry < counts_ref[0]).astype(jnp.int32)
        table[...] = jnp.zeros_like(table)
        for n, column in enumerate((block_row, listed - block_row * CB, live)):
            table[n : n + 1] = jnp.sum(jnp.where(hit, column, 0), axis=0, keepdims=True)
        copy = pltpu.make_async_copy(table, table_ref, load_sem.at[0])
        copy.start()
        copy.wait()

    def place(unit):
        q, fast, first, second, dh = unit
        return peer(first, second, dh) if fast == 0 else peer(second, first, dh)

    def unit_view(unit, half):
        source = place(unit)
        width = HALF if half is None else HALF // 2
        start = unit[1] * HALF + (half or 0) * width
        lines = pl.ds(pl.multiple_of(source % 2 * SHARD + unit[0] * UNIT, UNIT), UNIT)
        return rows.at[source // 2, lines, pl.ds(start, width)]

    def unit_sem(unit, half):
        q, fast, first, second, dh = unit
        if second == 2 or (first == 2 and second and half != (0 if second < 0 else 1)):
            return stay_recv.at[0]
        kind = [
            (-1, 0, None), (1, 0, None), (0, -1, None), (0, 1, None),
            (2, 0, 0), (2, 0, 1), (2, -1, 0), (2, 1, 1),
            (-1, -1, None), (-1, 1, None), (1, -1, None), (1, 1, None),
        ].index((first, second, half))
        return unit_recv.at[((q * 2 + dh) * 2 + fast) * 12 + kind]

    def unit_copy(unit, half, arrives, to):
        view = unit_view(unit, half)
        return pltpu.make_async_remote_copy(
            src_ref=view,
            dst_ref=view,
            send_sem=ring_send.at[0],
            recv_sem=unit_sem(arrives, half),
            device_id=(row, to),
            device_id_type=MESH,
        )

    def arrived(unit, half=None):
        unit_copy(unit, half, unit, col).wait_recv()

    def send(unit, axis, step, half=None):
        q, fast, first, second, dh = unit
        if axis == fast:
            first = (first - step + 1) % 4 - 1
        else:
            second = (second - step + 1) % 4 - 1
        to = peer(step, 0, 0) if axis == 0 else peer(0, step, 0)
        unit_copy(unit, half, (q, fast, first, second, dh), to).start()

    def both_ways(unit, axis, half=None):
        send(unit, axis, 1, half)
        send(unit, axis, -1, half)

    def forward(unit, axis, came):
        send(unit, axis, -came, 0 if came < 0 else 1)

    def pair_copy(q, source):
        lines = pl.ds(pl.multiple_of(source % 2 * SHARD + q * UNIT, UNIT), UNIT)
        view = rows.at[source // 2, lines]
        return pltpu.make_async_remote_copy(
            src_ref=view,
            dst_ref=view,
            send_sem=pair_send.at[0],
            recv_sem=pair_recv.at[q],
            device_id=(row, peer(0, 0, 1)),
            device_id_type=MESH,
        )

    def stage0(q, dh):
        if dh:
            pair_copy(q, peer(0, 0, 1)).wait_recv()
        for fast in (0, 1):
            both_ways((q, fast, 0, 0, dh), fast)
        for fast in (0, 1):
            both_ways((q, fast, 0, 0, dh), 1 - fast)

    def stage1(q, dh):
        for came in (-1, 1):
            for fast in (0, 1):
                unit = (q, fast, came, 0, dh)
                arrived(unit)
                forward(unit, fast, came)
                both_ways(unit, 1 - fast)

    def stage2(q, dh):
        for came in (-1, 1):
            for fast in (0, 1):
                unit = (q, fast, 0, came, dh)
                arrived(unit)
                forward(unit, 1 - fast, came)
        for half in (0, 1):
            for fast in (0, 1):
                unit = (q, fast, 2, 0, dh)
                arrived(unit, half)
                both_ways(unit, 1 - fast, half)

    def stage3(q, dh):
        for first in (-1, 1):
            for came in (-1, 1):
                for fast in (0, 1):
                    unit = (q, fast, first, came, dh)
                    arrived(unit)
                    forward(unit, 1 - fast, came)

    def stage4(q, dh):
        for came in (-1, 1):
            for fast in (0, 1):
                unit = (q, fast, 2, came, dh)
                arrived(unit, 0 if came < 0 else 1)
                forward(unit, 1 - fast, came)

    def panel_copy(part, slot, kind, to):
        first, last = PANEL_CUTS[part], PANEL_CUTS[part + 1]
        view = panels.at[slot, pl.ds(first, last - first)]
        return pltpu.make_async_remote_copy(
            src_ref=view,
            dst_ref=view,
            send_sem=panel_send.at[kind],
            recv_sem=panel_recv.at[part if kind == 0 else PANEL_PARTS + kind - 1],
            device_id=(to, col),
            device_id_type=MESH,
        )

    def start_panels():
        for part in range(PANEL_PARTS):
            panel_copy(part, row, 0, beside).start()

    def pass_panel(part):
        panel_copy(part, beside, 0, beside).wait_recv()
        panel_copy(part, beside, 2, other_core).start()

    load_rows.wait()
    for q in range(PARTS):
        pair_copy(q, col).start()
    for q in range(PARTS):
        stage0(q, 0)

    for load in loads:
        load.wait()
    fill_table()

    def masked(c, carry):
        column = pl.ds(pl.multiple_of(c * BS, BS), BS)
        for p in range(PB):
            factor = mask_ref[0, p, c].astype(jnp.float32)
            block = panel_in[p * BS : (p + 1) * BS, column]
            panels[row, c, p * BS : (p + 1) * BS] = (
                block.astype(jnp.float32) * factor
            ).astype(jnp.bfloat16)
        return carry

    lax.fori_loop(0, CB, masked, 0)
    for part in range(PANEL_PARTS):
        panel_copy(part, row, 1, other_core).start()
    stage1(0, 0)
    stage0(0, 1)
    start_panels()
    stage1(0, 1)
    stage2(0, 0)
    stage2(0, 1)
    stage3(0, 0)
    stage4(0, 0)
    stage3(0, 1)
    for part in range(PANEL_PARTS - 1):
        pass_panel(part)
    stage4(0, 1)
    pass_panel(PANEL_PARTS - 1)
    await_bytes(rows.at[pl.ds(0, 5)], stay_recv.at[0])
    await_bytes(panels.at[0], panel_recv.at[PANEL_PARTS])
    await_bytes(panels.at[0], panel_recv.at[PANEL_PARTS + 1])
    await_bytes(tile, tile_sem.at[0])

    def product(slot):
        i = table_ref[0, slot]
        j = table_ref[1, slot]
        live = table_ref[2, slot].astype(jnp.float32)
        cube = jnp.zeros((BS, BS), jnp.float32)
        for k in range(4):
            cube = cube + jnp.dot(
                rows[i, :, k * PB * BS : (k + 1) * PB * BS],
                panels[owners_ref[k], j],
                preferred_element_type=jnp.float32,
            )
        square = tile[j, i].astype(jnp.float32)
        return ((3.0 * square - 2.0 * cube) * live).astype(jnp.bfloat16)

    def owner_of(n):
        mixed = n * 5 % NCOL
        return peer(mixed // 8, mixed // 2 % 4, mixed % 2)

    def make(n):
        owner = owner_of(n)
        for s in range(SLOTS):
            staged[n, s] = product(owner * SLOTS + s)
        return owner

    mine = out_ref.at[pl.ds(col * SLOTS, SLOTS)]

    def give(n, owner):
        pltpu.make_async_remote_copy(
            src_ref=staged.at[n],
            dst_ref=mine,
            send_sem=out_send.at[0],
            recv_sem=out_recv.at[0],
            device_id=(row, owner),
            device_id_type=MESH,
        ).start()

    def exchange(pair, carry):
        n = 2 * pair + 2
        first, second = make(n), make(n + 1)
        give(n, first)
        give(n + 1, second)
        return carry

    give(1, make(1))
    lax.fori_loop(0, NCOL // 2 - 1, exchange, 0)
    make(0)
    keep = pltpu.make_async_copy(staged.at[0], mine, tile_sem.at[0])
    keep.start()

    await_bytes(rows.at[pl.ds(0, RB - 1)], ring_send.at[0])
    await_bytes(own, pair_send.at[0])
    for kind in range(3):
        await_bytes(panels.at[0], panel_send.at[kind])
    keep.wait()
    await_bytes(staged.at[pl.ds(1, NCOL - 1)], out_send.at[0])
    await_bytes(staged.at[pl.ds(1, NCOL - 1)], out_recv.at[0])


def shards(x2_rows, x_panels, panel_mask, owners, x2_tile, block_ids, dest, counts):
    sem = pltpu.SemaphoreType.DMA
    count = block_ids.shape[0]
    return pl.pallas_call(
        kernel,
        out_shape=jax.ShapeDtypeStruct((NCOL * SLOTS, BS, BS), jnp.bfloat16),
        in_specs=[pl.BlockSpec(memory_space=pltpu.HBM)] * 8,
        out_specs=pl.BlockSpec(memory_space=pl.ANY),
        scratch_shapes=[
            pltpu.VMEM((RB, BS, DEPTH), jnp.bfloat16),
            pltpu.VMEM((4, CB, PB * BS, BS), jnp.bfloat16),
            pltpu.VMEM((PB * BS, CB * BS), jnp.bfloat16),
            pltpu.VMEM((CB, RB, BS, BS), jnp.bfloat16),
            pltpu.VMEM((NCOL, SLOTS, BS, BS), jnp.bfloat16),
            pltpu.VMEM((1, count), jnp.int32),
            pltpu.VMEM((1, count), jnp.int32),
            pltpu.VMEM((8, BS), jnp.int32),
            pltpu.SMEM(counts.shape, jnp.int32),
            pltpu.SMEM(owners.shape, jnp.int32),
            pltpu.SMEM(panel_mask.shape, jnp.int32),
            pltpu.SMEM((8, BS), jnp.int32),
            sem((7,)),
            sem((1,)),
            sem((1,)),
            sem((1,)),
            sem((PARTS,)),
            sem((PARTS * 48,)),
            sem((1,)),
            sem((3,)),
            sem((PANEL_PARTS + 2,)),
            sem((1,)),
            sem((1,)),
        ],
        compiler_params=pltpu.CompilerParams(
            collective_id=0, has_side_effects=True, vmem_limit_bytes=60 * 2**20
        ),
        cost_estimate=pl.CostEstimate(
            flops=4_300_000_000, bytes_accessed=12_000_000, transcendentals=0
        ),
    )(
        block_ids.reshape(1, count),
        dest.reshape(1, count),
        counts,
        owners,
        panel_mask,
        x2_rows,
        x_panels,
        x2_tile.reshape(RB, BS, CB * BS),
    )


def solution(mesh):
    return jax.shard_map(
        shards,
        mesh=mesh,
        in_specs=(
            P(("row", "col"), None),
            P("row", None, "col"),
            P("row", None, "col"),
            P(),
            P("row", "col"),
            P(("row", "col")),
            P(("row", "col"), None),
            P(("row", "col")),
        ),
        out_specs=P(("row", "col"), None, None),
        check_vma=False,
    )
```

```python
import functools

import jax
import jax.numpy as jnp
from jax import lax
from jax.experimental import pallas as pl
from jax.experimental.pallas import tpu as pltpu
from jax.sharding import PartitionSpec as P

MESH = pl.DeviceIdType.MESH
BS = 128
CB = 11
RB = 16
PB = 4
DEPTH = 2048
HALF = DEPTH // 2
NCOL = 32
SHARD = 64
SLOTS = 2
PANEL_CUTS = (0, 3, 6, 9, 11)
PANEL_PARTS = len(PANEL_CUTS) - 1


def kernel(
    ids_hbm, dest_hbm, counts_hbm, owners_hbm, mask_hbm, rows_hbm, panel_hbm, tile_hbm, out_ref,
    rows, panels, panel_in, tile, staged, ids, dest, table,
    counts_ref, owners_ref, mask_ref, table_ref,
    load_sem, tile_sem, ring_send, pair_send, pair_recv, unit_recv, stay_recv, panel_send, panel_recv, out_send, out_recv,
):
    row = lax.axis_index("row")
    col = lax.axis_index("col")
    y, z, h = col // 8, (col // 2) % 4, col % 2
    x_lo, core = row // 2, row % 2

    def peer(dy, dz, dh):
        return ((y + dy + 4) % 4) * 8 + ((z + dz + 4) % 4) * 2 + (h + dh) % 2

    beside = (1 - x_lo) * 2 + core
    other_core = x_lo * 2 + 1 - core

    def shard(fast, source):
        lines = pl.ds(pl.multiple_of(source % 2 * SHARD, SHARD), SHARD)
        return rows.at[fast, source // 2, lines]

    load_rows = [
        pltpu.make_async_copy(
            rows_hbm.at[:, pl.ds(fast * HALF, HALF)], shard(fast, col), load_sem.at[fast]
        )
        for fast in (0, 1)
    ]
    for load in load_rows:
        load.start()

    barrier = pltpu.get_barrier_semaphore()

    def greet(n, carry):
        pl.semaphore_signal(
            barrier, inc=1, device_id=(row, (col + n) % NCOL), device_id_type=MESH
        )
        return carry

    lax.fori_loop(1, NCOL, greet, 0)
    pl.semaphore_signal(barrier, inc=1, device_id=(beside, col), device_id_type=MESH)
    pl.semaphore_signal(barrier, inc=1, device_id=(other_core, col), device_id_type=MESH)

    loads = [
        pltpu.make_async_copy(source, target, load_sem.at[n + 2])
        for n, (source, target) in enumerate(
            (
                (dest_hbm, dest),
                (ids_hbm, ids),
                (counts_hbm, counts_ref),
                (mask_hbm, mask_ref),
                (owners_hbm, owners_ref),
                (panel_hbm.at[0], panel_in),
            )
        )
    ]
    for load in loads:
        load.start()
    for c in range(CB):
        pltpu.make_async_copy(
            tile_hbm.at[:, :, pl.ds(c * BS, BS)], tile.at[c], tile_sem.at[0]
        ).start()
    pl.semaphore_wait(barrier, NCOL + 1)

    def await_bytes(ref, sem):
        pltpu.make_async_copy(ref, ref, sem).wait()

    def fill_table():
        count = ids.shape[1]
        first = lax.broadcasted_iota(jnp.int32, (count, count), 0)
        second = lax.broadcasted_iota(jnp.int32, (count, count), 1)

        def upright(line):
            return jnp.sum(jnp.where(first == second, line, 0), axis=1, keepdims=True)

        owner, listed = upright(dest[...]), upright(ids[...])
        before = (owner == dest[...]) & (second < first)
        slot = owner * SLOTS + jnp.sum(before.astype(jnp.int32), axis=1, keepdims=True)
        hit = slot == lax.broadcasted_iota(jnp.int32, (count, table.shape[1]), 1)
        block_row = (listed * 745) >> 13
        entry = lax.broadcasted_iota(jnp.int32, (count, 1), 0)
        live = (entry < counts_ref[0]).astype(jnp.int32)
        table[...] = jnp.zeros_like(table)
        for n, column in enumerate((block_row, listed - block_row * CB, live)):
            table[n : n + 1] = jnp.sum(jnp.where(hit, column, 0), axis=0, keepdims=True)
        copy = pltpu.make_async_copy(table, table_ref, load_sem.at[0])
        copy.start()
        copy.wait()

    def place(unit):
        fast, first, second, dh = unit
        return peer(first, second, dh) if fast == 0 else peer(second, first, dh)

    def unit_view(unit, half):
        view = shard(unit[0], place(unit))
        return view if half is None else view.at[pl.ds(half * SHARD // 2, SHARD // 2)]

    def unit_sem(unit, half):
        fast, first, second, dh = unit
        if second == 2 or (first == 2 and second and half != (0 if second < 0 else 1)):
            return stay_recv.at[0]
        kind = [
            (-1, 0, None), (1, 0, None), (0, -1, None), (0, 1, None),
            (2, 0, 0), (2, 0, 1), (2, -1, 0), (2, 1, 1),
            (-1, -1, None), (-1, 1, None), (1, -1, None), (1, 1, None),
        ].index((first, second, half))
        return unit_recv.at[(dh * 2 + fast) * 12 + kind]

    def unit_copy(unit, half, arrives, to):
        view = unit_view(unit, half)
        return pltpu.make_async_remote_copy(
            src_ref=view,
            dst_ref=view,
            send_sem=ring_send.at[0],
            recv_sem=unit_sem(arrives, half),
            device_id=(row, to),
            device_id_type=MESH,
        )

    def arrived(unit, half=None):
        unit_copy(unit, half, unit, col).wait_recv()

    def send(unit, axis, step, half=None):
        fast, first, second, dh = unit
        if axis == fast:
            first = (first - step + 1) % 4 - 1
        else:
            second = (second - step + 1) % 4 - 1
        to = peer(step, 0, 0) if axis == 0 else peer(0, step, 0)
        unit_copy(unit, half, (fast, first, second, dh), to).start()

    def both_ways(unit, axis, half=None):
        send(unit, axis, 1, half)
        send(unit, axis, -1, half)

    def forward(unit, axis, came):
        send(unit, axis, -came, 0 if came < 0 else 1)

    def pair_copy(fast, source):
        return pltpu.make_async_remote_copy(
            src_ref=shard(fast, source),
            dst_ref=shard(fast, source),
            send_sem=pair_send.at[0],
            recv_sem=pair_recv.at[fast],
            device_id=(row, peer(0, 0, 1)),
            device_id_type=MESH,
        )

    def stage0(dh):
        for fast in (0, 1):
            if dh:
                pair_copy(fast, peer(0, 0, 1)).wait_recv()
            both_ways((fast, 0, 0, dh), fast)
        for fast in (0, 1):
            both_ways((fast, 0, 0, dh), 1 - fast)

    def stage1(dh):
        for came in (-1, 1):
            for fast in (0, 1):
                unit = (fast, came, 0, dh)
                arrived(unit)
                forward(unit, fast, came)
                both_ways(unit, 1 - fast)

    def stage2(dh):
        for came in (-1, 1):
            for fast in (0, 1):
                unit = (fast, 0, came, dh)
                arrived(unit)
                forward(unit, 1 - fast, came)
        for half in (0, 1):
            for fast in (0, 1):
                unit = (fast, 2, 0, dh)
                arrived(unit, half)
                both_ways(unit, 1 - fast, half)

    def stage3(dh):
        for first in (-1, 1):
            for came in (-1, 1):
                for fast in (0, 1):
                    unit = (fast, first, came, dh)
                    arrived(unit)
                    forward(unit, 1 - fast, came)

    def stage4(dh):
        for came in (-1, 1):
            for fast in (0, 1):
                unit = (fast, 2, came, dh)
                arrived(unit, 0 if came < 0 else 1)
                forward(unit, 1 - fast, came)

    def panel_copy(part, slot, kind, to):
        first, last = PANEL_CUTS[part], PANEL_CUTS[part + 1]
        view = panels.at[slot, pl.ds(first, last - first)]
        return pltpu.make_async_remote_copy(
            src_ref=view,
            dst_ref=view,
            send_sem=panel_send.at[kind],
            recv_sem=panel_recv.at[part if kind == 0 else PANEL_PARTS + kind - 1],
            device_id=(to, col),
            device_id_type=MESH,
        )

    def start_panels():
        for part in range(PANEL_PARTS):
            panel_copy(part, row, 0, beside).start()

    def pass_panel(part):
        panel_copy(part, beside, 0, beside).wait_recv()
        panel_copy(part, beside, 2, other_core).start()

    for load in load_rows:
        load.wait()
    for fast in (0, 1):
        pair_copy(fast, col).start()
    stage0(0)

    for load in loads:
        load.wait()
    fill_table()

    def masked(c, carry):
        column = pl.ds(pl.multiple_of(c * BS, BS), BS)
        for p in range(PB):
            factor = mask_ref[0, p, c].astype(jnp.float32)
            block = panel_in[p * BS : (p + 1) * BS, column]
            panels[row, c, p * BS : (p + 1) * BS] = (
                block.astype(jnp.float32) * factor
            ).astype(jnp.bfloat16)
        return carry

    lax.fori_loop(0, CB, masked, 0)
    for part in range(PANEL_PARTS):
        panel_copy(part, row, 1, other_core).start()
    stage1(0)
    stage0(1)
    start_panels()
    stage1(1)
    stage2(0)
    stage2(1)
    stage3(0)
    stage4(0)
    stage3(1)
    for part in range(PANEL_PARTS - 1):
        pass_panel(part)
    stage4(1)
    pass_panel(PANEL_PARTS - 1)
    await_bytes(rows.at[0, pl.ds(0, 10)], stay_recv.at[0])
    await_bytes(panels.at[0], panel_recv.at[PANEL_PARTS])
    await_bytes(panels.at[0], panel_recv.at[PANEL_PARTS + 1])
    await_bytes(tile, tile_sem.at[0])

    def product(slot):
        i = table_ref[0, slot]
        j = table_ref[1, slot]
        live = table_ref[2, slot].astype(jnp.float32)
        cube = jnp.zeros((BS, BS), jnp.float32)
        for k in range(4):
            cube = cube + jnp.dot(
                rows[k // 2, i, :, k % 2 * PB * BS : (k % 2 + 1) * PB * BS],
                panels[owners_ref[k], j],
                preferred_element_type=jnp.float32,
            )
        square = tile[j, i].astype(jnp.float32)
        return ((3.0 * square - 2.0 * cube) * live).astype(jnp.bfloat16)

    def owner_of(n):
        mixed = n * 5 % NCOL
        return peer(mixed // 8, mixed // 2 % 4, mixed % 2)

    def make(n):
        owner = owner_of(n)
        for s in range(SLOTS):
            staged[n, s] = product(owner * SLOTS + s)
        return owner

    mine = out_ref.at[pl.ds(col * SLOTS, SLOTS)]

    def give(n, owner):
        pltpu.make_async_remote_copy(
            src_ref=staged.at[n],
            dst_ref=mine,
            send_sem=out_send.at[0],
            recv_sem=out_recv.at[0],
            device_id=(row, owner),
            device_id_type=MESH,
        ).start()

    def exchange(pair, carry):
        n = 2 * pair + 2
        first, second = make(n), make(n + 1)
        give(n, first)
        give(n + 1, second)
        return carry

    give(1, make(1))
    lax.fori_loop(0, NCOL // 2 - 1, exchange, 0)
    make(0)
    keep = pltpu.make_async_copy(staged.at[0], mine, tile_sem.at[0])
    keep.start()

    await_bytes(rows.at[:, pl.ds(0, RB - 1)], ring_send.at[0])
    await_bytes(rows.at[0, 0], pair_send.at[0])
    for kind in range(3):
        await_bytes(panels.at[0], panel_send.at[kind])
    keep.wait()
    await_bytes(staged.at[pl.ds(1, NCOL - 1)], out_send.at[0])
    await_bytes(staged.at[pl.ds(1, NCOL - 1)], out_recv.at[0])


def shards(x2_rows, x_panels, panel_mask, owners, x2_tile, block_ids, dest, counts):
    sem = pltpu.SemaphoreType.DMA
    count = block_ids.shape[0]
    return pl.pallas_call(
        kernel,
        out_shape=jax.ShapeDtypeStruct((NCOL * SLOTS, BS, BS), jnp.bfloat16),
        in_specs=[pl.BlockSpec(memory_space=pltpu.HBM)] * 8,
        out_specs=pl.BlockSpec(memory_space=pl.ANY),
        scratch_shapes=[
            pltpu.VMEM((2, RB, BS, HALF), jnp.bfloat16),
            pltpu.VMEM((4, CB, PB * BS, BS), jnp.bfloat16),
            pltpu.VMEM((PB * BS, CB * BS), jnp.bfloat16),
            pltpu.VMEM((CB, RB, BS, BS), jnp.bfloat16),
            pltpu.VMEM((NCOL, SLOTS, BS, BS), jnp.bfloat16),
            pltpu.VMEM((1, count), jnp.int32),
            pltpu.VMEM((1, count), jnp.int32),
            pltpu.VMEM((8, BS), jnp.int32),
            pltpu.SMEM(counts.shape, jnp.int32),
            pltpu.SMEM(owners.shape, jnp.int32),
            pltpu.SMEM(panel_mask.shape, jnp.int32),
            pltpu.SMEM((8, BS), jnp.int32),
            sem((8,)),
            sem((1,)),
            sem((1,)),
            sem((1,)),
            sem((2,)),
            sem((48,)),
            sem((1,)),
            sem((3,)),
            sem((PANEL_PARTS + 2,)),
            sem((1,)),
            sem((1,)),
        ],
        compiler_params=pltpu.CompilerParams(
            collective_id=0, has_side_effects=True, vmem_limit_bytes=60 * 2**20
        ),
        cost_estimate=pl.CostEstimate(
            flops=4_300_000_000, bytes_accessed=12_000_000, transcendentals=0
        ),
    )(
        block_ids.reshape(1, count),
        dest.reshape(1, count),
        counts,
        owners,
        panel_mask,
        x2_rows,
        x_panels,
        x2_tile.reshape(RB, BS, CB * BS),
    )


def solution(mesh):
    return jax.shard_map(
        shards,
        mesh=mesh,
        in_specs=(
            P(("row", "col"), None),
            P("row", None, "col"),
            P("row", None, "col"),
            P(),
            P("row", "col"),
            P(("row", "col")),
            P(("row", "col"), None),
            P(("row", "col")),
        ),
        out_specs=P(("row", "col"), None, None),
        check_vma=False,
    )
```

```python
import functools

import jax
import jax.numpy as jnp
from jax import lax
from jax.experimental import pallas as pl
from jax.experimental.pallas import tpu as pltpu
from jax.sharding import PartitionSpec as P

MESH = pl.DeviceIdType.MESH
BS = 128
CB = 11
RB = 16
PB = 4
DEPTH = 2048
HALF = DEPTH // 2
NCOL = 32
SHARD = 64
SLOTS = 2
PANEL_CUTS = (0, 3, 6, 9, 11)
PANEL_PARTS = len(PANEL_CUTS) - 1


def kernel(
    ids_hbm, dest_hbm, counts_hbm, owners_hbm, mask_hbm, rows_hbm, panel_hbm, tile_hbm, out_ref,
    rows, panels, panel_in, tile, staged, ids, dest, table,
    counts_ref, owners_ref, mask_ref, table_ref,
    load_sem, tile_sem, ring_send, pair_send, pair_recv, unit_recv, stay_recv, panel_send, panel_recv, out_send, out_recv,
):
    row = lax.axis_index("row")
    col = lax.axis_index("col")
    y, z, h = col // 8, (col // 2) % 4, col % 2
    x_lo, core = row // 2, row % 2

    def peer(dy, dz, dh):
        return ((y + dy + 4) % 4) * 8 + ((z + dz + 4) % 4) * 2 + (h + dh) % 2

    beside = (1 - x_lo) * 2 + core
    other_core = x_lo * 2 + 1 - core

    def shard(fast, source):
        lines = pl.ds(pl.multiple_of(source % 2 * SHARD, SHARD), SHARD)
        return rows.at[fast, source // 2, lines]

    load_rows = [
        pltpu.make_async_copy(
            rows_hbm.at[:, pl.ds(fast * HALF, HALF)], shard(fast, col), load_sem.at[fast]
        )
        for fast in (0, 1)
    ]
    for load in load_rows:
        load.start()

    barrier = pltpu.get_barrier_semaphore()

    def greet(n, carry):
        pl.semaphore_signal(
            barrier, inc=1, device_id=(row, (col + n) % NCOL), device_id_type=MESH
        )
        return carry

    lax.fori_loop(1, NCOL, greet, 0)
    pl.semaphore_signal(barrier, inc=1, device_id=(beside, col), device_id_type=MESH)
    pl.semaphore_signal(barrier, inc=1, device_id=(other_core, col), device_id_type=MESH)

    loads = [
        pltpu.make_async_copy(source, target, load_sem.at[n + 2])
        for n, (source, target) in enumerate(
            (
                (dest_hbm, dest),
                (ids_hbm, ids),
                (counts_hbm, counts_ref),
                (mask_hbm, mask_ref),
                (owners_hbm, owners_ref),
                (panel_hbm.at[0], panel_in),
            )
        )
    ]
    for load in loads:
        load.start()
    for c in range(CB):
        pltpu.make_async_copy(
            tile_hbm.at[:, :, pl.ds(c * BS, BS)], tile.at[c], tile_sem.at[0]
        ).start()
    pl.semaphore_wait(barrier, NCOL + 1)

    def await_bytes(ref, sem):
        pltpu.make_async_copy(ref, ref, sem).wait()

    def fill_table():
        count = ids.shape[1]
        first = lax.broadcasted_iota(jnp.int32, (count, count), 0)
        second = lax.broadcasted_iota(jnp.int32, (count, count), 1)

        def upright(line):
            return jnp.sum(jnp.where(first == second, line, 0), axis=1, keepdims=True)

        owner, listed = upright(dest[...]), upright(ids[...])
        before = (owner == dest[...]) & (second < first)
        slot = owner * SLOTS + jnp.sum(before.astype(jnp.int32), axis=1, keepdims=True)
        hit = slot == lax.broadcasted_iota(jnp.int32, (count, table.shape[1]), 1)
        block_row = (listed * 745) >> 13
        entry = lax.broadcasted_iota(jnp.int32, (count, 1), 0)
        live = (entry < counts_ref[0, 0]).astype(jnp.int32)
        table[...] = jnp.zeros_like(table)
        for n, column in enumerate((block_row, listed - block_row * CB, live)):
            table[n : n + 1] = jnp.sum(jnp.where(hit, column, 0), axis=0, keepdims=True)
        copy = pltpu.make_async_copy(table, table_ref, load_sem.at[0])
        copy.start()
        copy.wait()

    def place(unit):
        fast, first, second, dh = unit
        return peer(first, second, dh) if fast == 0 else peer(second, first, dh)

    def unit_view(unit, half):
        view = shard(unit[0], place(unit))
        return view if half is None else view.at[pl.ds(half * SHARD // 2, SHARD // 2)]

    def unit_sem(unit, half):
        fast, first, second, dh = unit
        if second == 2 or (first == 2 and second and half != (0 if second < 0 else 1)):
            return stay_recv.at[0]
        kind = [
            (-1, 0, None), (1, 0, None), (0, -1, None), (0, 1, None),
            (2, 0, 0), (2, 0, 1), (2, -1, 0), (2, 1, 1),
            (-1, -1, None), (-1, 1, None), (1, -1, None), (1, 1, None),
        ].index((first, second, half))
        return unit_recv.at[(dh * 2 + fast) * 12 + kind]

    def unit_copy(unit, half, arrives, to):
        view = unit_view(unit, half)
        return pltpu.make_async_remote_copy(
            src_ref=view,
            dst_ref=view,
            send_sem=ring_send.at[0],
            recv_sem=unit_sem(arrives, half),
            device_id=(row, to),
            device_id_type=MESH,
        )

    def arrived(unit, half=None):
        unit_copy(unit, half, unit, col).wait_recv()

    def send(unit, axis, step, half=None):
        fast, first, second, dh = unit
        if axis == fast:
            first = (first - step + 1) % 4 - 1
        else:
            second = (second - step + 1) % 4 - 1
        to = peer(step, 0, 0) if axis == 0 else peer(0, step, 0)
        unit_copy(unit, half, (fast, first, second, dh), to).start()

    def both_ways(unit, axis, half=None):
        send(unit, axis, 1, half)
        send(unit, axis, -1, half)

    def forward(unit, axis, came):
        send(unit, axis, -came, 0 if came < 0 else 1)

    def pair_copy(fast, source):
        return pltpu.make_async_remote_copy(
            src_ref=shard(fast, source),
            dst_ref=shard(fast, source),
            send_sem=pair_send.at[0],
            recv_sem=pair_recv.at[fast],
            device_id=(row, peer(0, 0, 1)),
            device_id_type=MESH,
        )

    def stage0(dh):
        for fast in (0, 1):
            if dh:
                pair_copy(fast, peer(0, 0, 1)).wait_recv()
            both_ways((fast, 0, 0, dh), fast)
        for fast in (0, 1):
            both_ways((fast, 0, 0, dh), 1 - fast)

    def stage1(dh):
        for came in (-1, 1):
            for fast in (0, 1):
                unit = (fast, came, 0, dh)
                arrived(unit)
                forward(unit, fast, came)
                both_ways(unit, 1 - fast)

    def stage2(dh):
        for came in (-1, 1):
            for fast in (0, 1):
                unit = (fast, 0, came, dh)
                arrived(unit)
                forward(unit, 1 - fast, came)
        for half in (0, 1):
            for fast in (0, 1):
                unit = (fast, 2, 0, dh)
                arrived(unit, half)
                both_ways(unit, 1 - fast, half)

    def stage3(dh):
        for first in (-1, 1):
            for came in (-1, 1):
                for fast in (0, 1):
                    unit = (fast, first, came, dh)
                    arrived(unit)
                    forward(unit, 1 - fast, came)

    def stage4(dh):
        for came in (-1, 1):
            for fast in (0, 1):
                unit = (fast, 2, came, dh)
                arrived(unit, 0 if came < 0 else 1)
                forward(unit, 1 - fast, came)

    def panel_copy(part, slot, kind, to):
        first, last = PANEL_CUTS[part], PANEL_CUTS[part + 1]
        view = panels.at[slot, pl.ds(first, last - first)]
        return pltpu.make_async_remote_copy(
            src_ref=view,
            dst_ref=view,
            send_sem=panel_send.at[kind],
            recv_sem=panel_recv.at[part if kind == 0 else PANEL_PARTS + kind - 1],
            device_id=(to, col),
            device_id_type=MESH,
        )

    def start_panels():
        for part in range(PANEL_PARTS):
            panel_copy(part, row, 0, beside).start()

    def pass_panel(part):
        panel_copy(part, beside, 0, beside).wait_recv()
        panel_copy(part, beside, 2, other_core).start()

    for load in load_rows:
        load.wait()
    for fast in (0, 1):
        pair_copy(fast, col).start()
    stage0(0)

    for load in loads:
        load.wait()
    fill_table()

    def masked(c, carry):
        column = pl.ds(pl.multiple_of(c * BS, BS), BS)
        for p in range(PB):
            factor = mask_ref[0, p, c].astype(jnp.float32)
            block = panel_in[p * BS : (p + 1) * BS, column]
            panels[row, c, p * BS : (p + 1) * BS] = (
                block.astype(jnp.float32) * factor
            ).astype(jnp.bfloat16)
        return carry

    lax.fori_loop(0, CB, masked, 0)
    for part in range(PANEL_PARTS):
        panel_copy(part, row, 1, other_core).start()
    stage1(0)
    stage0(1)
    start_panels()
    stage1(1)
    stage2(0)
    stage2(1)
    stage3(0)
    stage4(0)
    stage3(1)
    for part in range(PANEL_PARTS - 1):
        pass_panel(part)
    stage4(1)
    pass_panel(PANEL_PARTS - 1)
    await_bytes(rows.at[0, pl.ds(0, 10)], stay_recv.at[0])
    await_bytes(panels.at[0], panel_recv.at[PANEL_PARTS])
    await_bytes(panels.at[0], panel_recv.at[PANEL_PARTS + 1])
    await_bytes(tile, tile_sem.at[0])

    def product(slot):
        i = table_ref[0, slot]
        j = table_ref[1, slot]
        live = table_ref[2, slot].astype(jnp.float32)
        cube = jnp.zeros((BS, BS), jnp.float32)
        for k in range(4):
            cube = cube + jnp.dot(
                rows[k // 2, i, :, k % 2 * PB * BS : (k % 2 + 1) * PB * BS],
                panels[owners_ref[k], j],
                preferred_element_type=jnp.float32,
            )
        square = tile[j, i].astype(jnp.float32)
        return ((3.0 * square - 2.0 * cube) * live).astype(jnp.bfloat16)

    def owner_of(n):
        mixed = n * 5 % NCOL
        return peer(mixed // 8, mixed // 2 % 4, mixed % 2)

    def make(n):
        owner = owner_of(n)
        for s in range(SLOTS):
            staged[n, s] = product(owner * SLOTS + s)
        return owner

    mine = out_ref.at[pl.ds(col * SLOTS, SLOTS)]

    def give(n, owner):
        pltpu.make_async_remote_copy(
            src_ref=staged.at[n],
            dst_ref=mine,
            send_sem=out_send.at[0],
            recv_sem=out_recv.at[0],
            device_id=(row, owner),
            device_id_type=MESH,
        ).start()

    def exchange(pair, carry):
        n = 2 * pair + 2
        first, second = make(n), make(n + 1)
        give(n, first)
        give(n + 1, second)
        return carry

    give(1, make(1))
    lax.fori_loop(0, NCOL // 2 - 1, exchange, 0)
    make(0)
    keep = pltpu.make_async_copy(staged.at[0], mine, tile_sem.at[0])
    keep.start()

    await_bytes(rows.at[:, pl.ds(0, RB - 1)], ring_send.at[0])
    await_bytes(rows.at[0, 0], pair_send.at[0])
    for kind in range(3):
        await_bytes(panels.at[0], panel_send.at[kind])
    keep.wait()
    await_bytes(staged.at[pl.ds(1, NCOL - 1)], out_send.at[0])
    await_bytes(staged.at[pl.ds(1, NCOL - 1)], out_recv.at[0])


def shards(x2_rows, x_panels, panel_mask, owners, x2_tile, block_ids, dest, counts):
    sem = pltpu.SemaphoreType.DMA
    count = block_ids.shape[0]
    return pl.pallas_call(
        kernel,
        out_shape=jax.ShapeDtypeStruct((NCOL * SLOTS, BS, BS), jnp.bfloat16),
        in_specs=[pl.BlockSpec(memory_space=pltpu.HBM)] * 8,
        out_specs=pl.BlockSpec(memory_space=pl.ANY),
        scratch_shapes=[
            pltpu.VMEM((2, RB, BS, HALF), jnp.bfloat16),
            pltpu.VMEM((4, CB, PB * BS, BS), jnp.bfloat16),
            pltpu.VMEM((PB * BS, CB * BS), jnp.bfloat16),
            pltpu.VMEM((CB, RB, BS, BS), jnp.bfloat16),
            pltpu.VMEM((NCOL, SLOTS, BS, BS), jnp.bfloat16),
            pltpu.VMEM((1, count), jnp.int32),
            pltpu.VMEM((1, count), jnp.int32),
            pltpu.VMEM((8, BS), jnp.int32),
            pltpu.SMEM((1, 1), jnp.int32),
            pltpu.SMEM(owners.shape, jnp.int32),
            pltpu.SMEM(panel_mask.shape, jnp.int32),
            pltpu.SMEM((8, BS), jnp.int32),
            sem((8,)),
            sem((1,)),
            sem((1,)),
            sem((1,)),
            sem((2,)),
            sem((48,)),
            sem((1,)),
            sem((3,)),
            sem((PANEL_PARTS + 2,)),
            sem((1,)),
            sem((1,)),
        ],
        compiler_params=pltpu.CompilerParams(
            collective_id=0, has_side_effects=True, vmem_limit_bytes=60 * 2**20
        ),
        cost_estimate=pl.CostEstimate(
            flops=4_300_000_000, bytes_accessed=12_000_000, transcendentals=0
        ),
    )(
        block_ids.reshape(1, count),
        dest.reshape(1, count),
        counts.reshape(1, 1),
        owners,
        panel_mask,
        x2_rows,
        x_panels,
        x2_tile.reshape(RB, BS, CB * BS),
    )


def solution(mesh):
    return jax.shard_map(
        shards,
        mesh=mesh,
        in_specs=(
            P(("row", "col"), None),
            P("row", None, "col"),
            P("row", None, "col"),
            P(),
            P("row", "col"),
            P(("row", "col")),
            P(("row", "col"), None),
            P(("row", "col")),
        ),
        out_specs=P(("row", "col"), None, None),
        check_vma=False,
    )
```
